32 devices in a mesh: batch: 4 (over y, x), train: 8 (over z, core).
Axes of the slice: x: 2, y: 2, z: 4, core: 2. Of those that a mesh axis runs over, the one named last changes fastest.
Arguments:
- batch_rows: int32 [2, 4096], replicated, may hold values from 0 to 32767, as said below
- train_embed: bfloat16 [32768, 256], P('train'), may hold values from -6 to 6
- lib_embed: bfloat16 [4096, 256], P('batch'), may hold values from -6 to 6
- labels: float32 [32768], P('train'), may hold values from -6 to 6
- prior_draws: float32 [32, 32768], P(None, 'train'), may hold values from -6 to 6
- noise_draws: float32 [32, 32768], P(None, 'train'), may hold values from -6 to 6
- coefficients: float32 [33, 32768], P(None, 'train'), may hold values from -4 to 4
- velocity: float32 [33, 32768], P(None, 'train'), may hold values from -1.6 to 1.6
- library_prior: float32 [32, 4096], P(None, ('batch', 'train')), may hold values from -6 to 6
Outputs:
- new_coefficients: float32 [33, 32768], P(None, 'train')
- new_velocity: float32 [33, 32768], P(None, 'train')
- predictions: float32 [33, 4096], P(None, ('batch', 'train'))
The draws below stay inside these ranges and needn't reach their ends.
Inputs may be any that keep to these rules, and one draw needn't show every extreme that they name: `batch_rows`: each step's 4096 rows are distinct. A step's positions fall into runs of 128; run number q holds rows of the range starting at (q % 8) * 4096 of length 4096.
All inputs are finite; a program needn't handle non-finite values.
Results may differ from the reference program's by a relative error of at most 0.009.
Values may be sent and summed in bfloat16 or wider, within the bound.
A program may use at most 64 MiB of HBM per device.

```python
import jax
import jax.numpy as jnp
from jax import lax

D = 256
SAMPLES = 32
STEPS = 2
TRAIN_DEV = 4096
BATCH_DEV = 1024
N = 32768
BATCH = 4096
LIBRARY = 4096
OWN = 128
COLS = 33
CLUSTERS = 512
N_TRAIN = 8


def family_centers(key):
    return jax.random.normal(jax.random.fold_in(key, 7), (CLUSTERS, D), jnp.float32)


def clustered(key, salt, count):
    centers = family_centers(key)
    member = jax.random.randint(jax.random.fold_in(key, salt), (count,), 0, CLUSTERS)
    spread = 0.315 * jax.random.normal(jax.random.fold_in(key, salt + 1), (count, D), jnp.float32)
    rows = jnp.take(centers, member, axis=0) + spread
    return jnp.clip(rows, -6.0, 6.0).astype(jnp.bfloat16)


def draw_train_embed(key, part):
    return clustered(key, 21, N)


def draw_lib_embed(key, part):
    return clustered(key, 31, LIBRARY)


def draw_batch_rows(key, part):
    shards = N // TRAIN_DEV
    groups = BATCH // BATCH_DEV
    picked_count = groups * OWN

    def one_step(step_index):
        step_key = jax.random.fold_in(key, 100 + step_index)

        def one_shard(shard):
            order = jax.random.permutation(jax.random.fold_in(step_key, shard), TRAIN_DEV)
            return order[:picked_count].reshape(groups, OWN) + shard * TRAIN_DEV
        table = jax.vmap(one_shard)(jnp.arange(shards, dtype=jnp.int32))
        return jnp.transpose(table, (1, 0, 2)).reshape(BATCH)
    return jnp.stack([one_step(step_index) for step_index in range(STEPS)]).astype(jnp.int32)


def shard_levels(own_key, extent, cuts, smallest, top_value):
    def one(axis_at, shards_of):
        steps = jax.random.uniform(jax.random.fold_in(jax.random.fold_in(own_key, 6), axis_at), (shards_of,), jnp.float32, smallest / len(cuts), top_value / len(cuts))
        return jnp.repeat(jnp.exp(steps), extent[axis_at] // shards_of).reshape((-1,) + (1,) * (len(extent) - axis_at - 1))

    loudness = one(*cuts[0])
    for cut in cuts[1:]:
        loudness = loudness * one(*cut)
    return loudness


def gaussian(rng, shape, scale, limit, cuts=(), kind=jnp.bfloat16):
    gain = shard_levels(rng, shape, cuts, -0.22, 0.18) if cuts else 1.0
    values = jax.random.normal(rng, shape, jnp.float32) * scale * gain
    return jnp.minimum(jnp.maximum(values, -limit), limit).astype(kind)


def setup_inputs(seed: int = 0) -> dict:
    splits = jax.random.split(jax.random.key(seed), 10)
    return {
        "batch_rows": draw_batch_rows(jax.random.fold_in(splits[9], 71), 0),
        "train_embed": draw_train_embed(jax.random.fold_in(splits[9], 71), 0),
        "lib_embed": draw_lib_embed(jax.random.fold_in(splits[9], 71), 0),
        "labels": gaussian(splits[3], (N,), 1.0, 6.0, ((0, 8),), jnp.float32),
        "prior_draws": gaussian(splits[4], (SAMPLES, N), 1.0, 6.0, ((1, 8),), jnp.float32),
        "noise_draws": gaussian(splits[5], (SAMPLES, N), 1.0, 6.0, ((1, 8),), jnp.float32),
        "coefficients": gaussian(splits[6], (COLS, N), 0.5, 4.0, ((1, 8),), jnp.float32),
        "velocity": gaussian(splits[7], (COLS, N), 0.2, 1.6, ((1, 8),), jnp.float32),
        "library_prior": gaussian(splits[8], (SAMPLES, LIBRARY), 1.0, 6.0, ((1, 32),), jnp.float32),
    }


momentum = 0.9
step_rate = 0.1
noise_var = 0.5
noise_scale = 0.7071067811865476
length_sq = 0.088

def contract_rows(left, right):
    return lax.dot_general(left, right, (((1,), (1,)), ((), ())), preferred_element_type=jnp.float32)

def kernel_tile(query, keys, key_norms, width):
    query_norms = lax.optimization_barrier(jnp.sum(jnp.square(query.astype(jnp.float32)), axis=1))
    cross = contract_rows(query, keys)
    dist = query_norms[:, None] + key_norms[None, :] - 2.0 * cross
    scaled = jnp.sqrt(5.0 * jnp.maximum(dist, 0.0) / (length_sq * width))
    return ((1.0 + scaled + scaled * scaled / 3.0) * jnp.exp(-scaled)).astype(jnp.bfloat16)

def apply_kernel(query, train_embed, weights):
    width = train_embed.shape[1]
    key_norms = lax.optimization_barrier(jnp.sum(jnp.square(train_embed.astype(jnp.float32)), axis=1))
    systems = weights.shape[0]

    def one_block(carry, parts):
        keys, norms, block_weights = parts
        tile = kernel_tile(query, keys, norms, width)
        return (carry + contract_rows(block_weights, tile), None)
    start = jnp.zeros((systems, query.shape[0]), jnp.float32)
    total, _ = lax.scan(one_block, start, (train_embed.reshape(N_TRAIN, TRAIN_DEV, width), key_norms.reshape(N_TRAIN, TRAIN_DEV), jnp.transpose(weights.reshape(systems, N_TRAIN, TRAIN_DEV), (1, 0, 2))))
    return total

def reference(batch_rows, train_embed, lib_embed, labels, prior_draws, noise_draws, coefficients, velocity, library_prior):
    targets = jnp.concatenate([labels[None, :], labels[None, :] - prior_draws - noise_scale * noise_draws], axis=0)
    for step_index in range(STEPS):
        chosen = batch_rows[step_index]
        ahead = coefficients + momentum * velocity
        query = jnp.take(train_embed, chosen, axis=0)
        resid = apply_kernel(query, train_embed, ahead.astype(jnp.bfloat16))
        resid = resid + noise_var * jnp.take(ahead, chosen, axis=1) - jnp.take(targets, chosen, axis=1)
        grad = jnp.zeros_like(coefficients).at[:, chosen].add(resid)
        velocity = momentum * velocity - step_rate * grad
        coefficients = coefficients + velocity
    predicted = apply_kernel(lib_embed, train_embed, coefficients.astype(jnp.bfloat16))
    shifts = jnp.concatenate([jnp.zeros((1, predicted.shape[1]), jnp.float32), library_prior], axis=0)
    return (coefficients, velocity, predicted + shifts)
```

```python
import functools
import math

import jax
import jax.numpy as jnp
from jax import lax
from jax.experimental import pallas as pl
from jax.experimental.pallas import tpu as pltpu
from jax.sharding import PartitionSpec as P

momentum = 0.9
step_rate = 0.1
noise_var = 0.5
noise_scale = 0.7071067811865476
length_sq = 0.088

f32 = jnp.float32
bf16 = jnp.bfloat16
BLOCK = 256


def dot(a, b):
    return lax.dot_general(a, b, (((1,), (0,)), ((), ())), preferred_element_type=f32)


def dot_t(a, b):
    return lax.dot_general(a, b, (((1,), (1,)), ((), ())), preferred_element_type=f32)


def body(
    T, B, COLS,
    rows_ref, embed_hbm, lib_hbm, labels_hbm, prior_hbm, noise_hbm, coef_hbm, vel_hbm, shift_ref,
    newc_hbm, newv_hbm, pred_ref,
    embed, lib, labels, prior, noise, coef, vel, outc, outv,
    norms, hot0, hot1, wide, targets, w_first, w_base,
    qbuf, qt, acc, acc_lib, keys0, keys1, part2, part_l0, part_l1, overlap, own_terms,
    rs_send, rs_recv, rl_send, rl_recv, ag, gall,
    in_sem, out_sem, q_send, q_recv, f_send, f_recv, rs_ss, rs_rs, ag_ss, ag_rs,
):
    t = lax.axis_index("train")
    b = lax.axis_index("batch")
    R, D = embed.shape
    CP = acc.shape[0]
    O = ag.shape[3]
    OL = rl_send.shape[2]
    H = T // 2
    hots = (hot0, hot1)
    alpha = math.sqrt(5.0 / (length_sq * D))
    gamma = alpha * math.log2(math.e)
    c1 = 1.5 / alpha
    c2 = 0.75 / (alpha * alpha)
    kappa = alpha * alpha / 3.0

    ins = []
    for i, (src, dst) in enumerate(
        (
            (embed_hbm, embed), (lib_hbm, lib), (coef_hbm, coef), (vel_hbm, vel),
            (labels_hbm, labels), (prior_hbm, prior), (noise_hbm, noise),
        )
    ):
        copy = pltpu.make_async_copy(src, dst, in_sem.at[i])
        copy.start()
        ins.append(copy)

    barrier = pltpu.get_barrier_semaphore()
    for d in range(1, T):
        pl.semaphore_signal(
            barrier, inc=1, device_id={"train": lax.rem(t + d, T)},
            device_id_type=pl.DeviceIdType.MESH,
        )
    for d in range(1, B):
        pl.semaphore_signal(
            barrier, inc=1, device_id={"batch": lax.rem(b + d, B)},
            device_id_type=pl.DeviceIdType.MESH,
        )

    base_row = (t * R).astype(f32)
    diagonal = lax.broadcasted_iota(jnp.int32, (O, O), 0) == lax.broadcasted_iota(
        jnp.int32, (O, O), 1
    )

    def build_hot(s, d):
        group = lax.rem(b + B - d, B)
        run = rows_ref[pl.ds(s * (B * T) + group * T + t, 1), :].astype(f32) - base_row
        column = jnp.sum(jnp.where(diagonal, run, 0.0), axis=1, keepdims=True).astype(jnp.int32)
        lane = lax.broadcasted_iota(jnp.int32, (O, R), 1)
        hots[s][d * O : (d + 1) * O, :] = jnp.where(column == lane, 1.0, 0.0).astype(bf16)

    def remote(src, dst, ss, rs, axis, peer):
        return pltpu.make_async_remote_copy(
            src_ref=src, dst_ref=dst, send_sem=ss, recv_sem=rs,
            device_id={axis: peer}, device_id_type=pl.DeviceIdType.MESH,
        )

    sibling = t + 1 - 2 * lax.rem(t, 2)
    sends = []

    def q_direct(s, d):
        return remote(
            qbuf.at[s, t], qbuf.at[s, t], q_send.at[s, d], q_recv.at[s, d],
            "train", lax.rem(t + 2 * d, T),
        )

    def q_direct_recv(s, d):
        slot = lax.rem(t + T - 2 * d, T)
        remote(
            qbuf.at[s, slot], qbuf.at[s, slot], q_send.at[s, d], q_recv.at[s, d],
            "train", slot,
        ).wait_recv()

    def q_forward(s, d):
        slot = lax.rem(t + T - 2 * d, T)
        return remote(
            qbuf.at[s, slot], qbuf.at[s, slot], f_send.at[s, d], f_recv.at[s, d],
            "train", sibling,
        )

    def q_forward_recv(s, d):
        slot = lax.rem(sibling + T - 2 * d, T)
        remote(
            qbuf.at[s, slot], qbuf.at[s, slot], f_send.at[s, d], f_recv.at[s, d],
            "train", sibling,
        ).wait_recv()

    def start(copy):
        copy.start()
        sends.append(copy)

    def send_queries(s):
        for d in range(1, H):
            start(q_direct(s, d))
        start(q_forward(s, 0))

    def forward_queries(s):
        for d in range(1, H):
            q_direct_recv(s, d)
            start(q_forward(s, d))

    def finish_queries(s):
        for d in range(H):
            q_forward_recv(s, d)

    build_hot(0, 0)
    build_hot(1, 0)
    ins[0].wait()
    for s in range(2):
        qbuf[s, t] = dot(hots[s][0:O, :], embed[...]).astype(bf16)
    pl.semaphore_wait(barrier, T - 1 + B - 1)
    send_queries(0)

    def norm_block(i, _):
        at = pl.ds(pl.multiple_of(i * BLOCK, BLOCK), BLOCK)
        x = embed[at, :].astype(f32)
        norms[at, :] = jnp.broadcast_to(jnp.sum(x * x, axis=1, keepdims=True), (BLOCK, 128))
        return 0

    lax.fori_loop(0, R // BLOCK, norm_block, 0)

    ins[2].wait()
    ins[3].wait()
    wide[COLS - 1 : CP, :] = jnp.zeros((CP - COLS + 1, R), f32)
    wide[0:COLS, :] = coef[...] + momentum * (1.0 + momentum) * vel[...]
    w_base[...] = wide[...].astype(bf16)

    def query_side(q):
        qf = q.astype(f32).T
        qt[...] = (-2.0 * qf).astype(bf16)
        return jnp.sum(qf * qf, axis=0, keepdims=True)

    def kernel_block(keys, key_norms, query_norms):
        Q = query_norms.shape[1]
        wide_norms = jnp.concatenate([key_norms] * (Q // 128), axis=1)
        dist = jnp.maximum(dot(keys, qt[...]) + query_norms + wide_norms, 1e-20)
        root = dist * lax.rsqrt(dist)
        shifted = root + c1
        return ((shifted * shifted + c2) * jnp.exp2(root * (-gamma))).astype(bf16)

    def apply_blocks(lower, upper, weights, query_norms, total):
        def step(i, _):
            at = pl.ds(pl.multiple_of(i * BLOCK, BLOCK), BLOCK)
            tile = kernel_block(embed[at, :], norms[at, :], query_norms)
            total[...] += dot(weights[:, at], tile)
            return 0

        lax.fori_loop(lower, upper, step, 0)

    def compact(keys, out, query_norms):
        x = keys[...].astype(f32)
        key_norms = jnp.broadcast_to(jnp.sum(x * x, axis=1, keepdims=True), (x.shape[0], 128))
        size = min(BLOCK, x.shape[0])
        for i in range(x.shape[0] // size):
            at = slice(i * size, (i + 1) * size)
            out[at, :] = kernel_block(keys[at, :], key_norms[at, :], query_norms)

    def scatter_send(ph, value):
        send, recv, size = (rs_send.at[ph], rs_recv.at[ph], O) if ph < 2 else (rl_send, rl_recv, OL)
        for k in range(T):
            send[k] = value[:, k * size : (k + 1) * size].astype(bf16)
        for d in range(1, T):
            peer = lax.rem(t + d, T)
            start(
                remote(
                    send.at[peer], recv.at[d - 1], rs_ss.at[ph, d], rs_rs.at[ph, d], "train", peer
                )
            )

    def scatter_recv(ph):
        send, recv = (rs_send.at[ph], rs_recv.at[ph]) if ph < 2 else (rl_send, rl_recv)
        total = send[t].astype(f32)
        for d in range(1, T):
            remote(
                send.at[0], recv.at[d - 1], rs_ss.at[ph, d], rs_rs.at[ph, d],
                "train", lax.rem(t + d, T),
            ).wait_recv()
            total = total + recv[d - 1].astype(f32)
        return total

    def share(ph, value):
        ag[ph, 0] = value.astype(bf16)
        for d in range(1, B):
            start(
                remote(
                    ag.at[ph, 0], ag.at[ph, d], ag_ss.at[ph, d], ag_rs.at[ph, d],
                    "batch", lax.rem(b + d, B),
                )
            )

    def collect(ph):
        for d in range(1, B):
            remote(
                ag.at[ph, 0], ag.at[ph, d], ag_ss.at[ph, d], ag_rs.at[ph, d],
                "batch", lax.rem(b + d, B),
            ).wait_recv()
        for d in range(B):
            gall[ph, :, d * O : (d + 1) * O] = ag[ph, d]

    blocks = R // BLOCK
    half = blocks // 2

    ins[1].wait()
    acc_lib[...] = jnp.zeros_like(acc_lib)
    lib_norms = query_side(lib[...])
    apply_blocks(0, half // 2, w_base, lib_norms, acc_lib)

    ins[4].wait()
    ins[5].wait()
    ins[6].wait()
    targets[COLS - 1 : CP, :] = jnp.zeros((CP - COLS + 1, R), f32)
    targets[0:1, :] = labels[...]
    targets[1:COLS, :] = labels[...] - prior[...] - noise_scale * noise[...]

    def own_term(s):
        value = noise_var * wide[...] - targets[...]
        high = value.astype(bf16)
        low = (value - high.astype(f32)).astype(bf16)
        own = hots[s][0:O, :]
        own_terms[s] = dot_t(high, own) + dot_t(low, own)

    own_term(1)
    wide[0:COLS, :] = coef[...] + momentum * vel[...]
    w_first[...] = wide[...].astype(bf16)
    own_term(0)
    for d in range(1, B):
        build_hot(0, d)
    keys0[...] = dot(hot0[...], embed[...]).astype(bf16)
    overlap[...] = dot_t(hot0[...], hot1[0:O, :]).astype(bf16)

    forward_queries(0)
    send_queries(1)
    apply_blocks(half // 2, half, w_base, lib_norms, acc_lib)
    finish_queries(0)

    acc[...] = jnp.zeros_like(acc)
    first_norms = query_side(qbuf[0].reshape(T * O, D))
    apply_blocks(0, blocks, w_first, first_norms, acc)
    scatter_send(0, kappa * acc[...])
    forward_queries(1)
    for d in range(1, B):
        build_hot(1, d)
    keys1[...] = dot(hot1[...], embed[...]).astype(bf16)
    finish_queries(1)

    acc[...] = jnp.zeros_like(acc)
    second_norms = query_side(qbuf[1].reshape(T * O, D))
    apply_blocks(0, half, w_base, second_norms, acc)
    share(0, scatter_recv(0) + own_terms[0])
    apply_blocks(half, blocks, w_base, second_norms, acc)
    compact(keys0, part2, second_norms)
    collect(0)
    g0 = gall[0]
    look = step_rate * (1.0 + momentum)
    scatter_send(1, kappa * (acc[...] - look * dot(g0, part2[...])))
    own_terms[1] = own_terms[1] - (noise_var * look) * dot(g0, overlap[...])

    lib_norms = query_side(lib[...])
    mid = half + half // 2
    apply_blocks(half, mid, w_base, lib_norms, acc_lib)
    share(1, scatter_recv(1) + own_terms[1])
    apply_blocks(mid, blocks, w_base, lib_norms, acc_lib)
    compact(keys0, part_l0, lib_norms)
    compact(keys1, part_l1, lib_norms)
    acc_lib[...] -= look * dot(g0, part_l0[...])
    collect(1)
    g1 = gall[1]
    scatter_send(2, kappa * (acc_lib[...] - step_rate * dot(g1, part_l1[...])))

    CH = min(R, 1024)
    for i in range(R // CH):
        at = slice(i * CH, (i + 1) * CH)
        grad0 = dot(g0, hot0[:, at])[0:COLS]
        grad1 = dot(g1, hot1[:, at])[0:COLS]
        v1 = momentum * vel[:, at] - step_rate * grad0
        v2 = momentum * v1 - step_rate * grad1
        outv[:, at] = v2
        outc[:, at] = (coef[:, at] + v1) + v2
    out_c = pltpu.make_async_copy(outc, newc_hbm, out_sem.at[0])
    out_v = pltpu.make_async_copy(outv, newv_hbm, out_sem.at[1])
    out_c.start()
    out_v.start()

    total = scatter_recv(2)
    pred_ref[0:1, :] = total[0:1]
    pred_ref[1:COLS, :] = total[1:COLS] + shift_ref[...]
    out_c.wait()
    out_v.wait()
    for copy in sends:
        copy.wait_send()


def per_device(
    T, B,
    batch_rows, train_embed, lib_embed, labels, prior_draws, noise_draws,
    coefficients, velocity, library_prior,
):
    steps, batch = batch_rows.shape
    O = batch // (B * T)
    R, D = train_embed.shape
    COLS = coefficients.shape[0]
    CP = -(-COLS // 16) * 16
    LQ = lib_embed.shape[0]
    OL = LQ // T
    Q = T * O
    vmem = lambda *shape, dtype=f32: pltpu.VMEM(shape, dtype)
    dma = lambda *shape: pltpu.SemaphoreType.DMA(shape)
    whole = pl.BlockSpec(memory_space=pltpu.VMEM)
    far = pl.BlockSpec(memory_space=pl.ANY)
    scratch = [
        vmem(R, D, dtype=bf16), vmem(LQ, D, dtype=bf16), vmem(1, R), vmem(COLS - 1, R),
        vmem(COLS - 1, R), vmem(COLS, R), vmem(COLS, R), vmem(COLS, R), vmem(COLS, R),
        vmem(R, 128), vmem(B * O, R, dtype=bf16), vmem(B * O, R, dtype=bf16),
        vmem(CP, R), vmem(CP, R), vmem(CP, R, dtype=bf16), vmem(CP, R, dtype=bf16),
        vmem(2, T, O, D, dtype=bf16), vmem(D, Q, dtype=bf16), vmem(CP, Q), vmem(CP, LQ),
        vmem(B * O, D, dtype=bf16), vmem(B * O, D, dtype=bf16),
        vmem(B * O, Q, dtype=bf16), vmem(B * O, LQ, dtype=bf16), vmem(B * O, LQ, dtype=bf16),
        vmem(B * O, O, dtype=bf16), vmem(2, CP, O),
        vmem(2, T, CP, O, dtype=bf16), vmem(2, T - 1, CP, O, dtype=bf16),
        vmem(T, CP, OL, dtype=bf16), vmem(T - 1, CP, OL, dtype=bf16),
        vmem(2, B, CP, O, dtype=bf16), vmem(2, CP, B * O, dtype=bf16),
        dma(7), dma(2), dma(2, T), dma(2, T), dma(2, T), dma(2, T),
        dma(3, T), dma(3, T), dma(2, B), dma(2, B),
    ]
    pairs = (2 * Q + LQ) * R
    return pl.pallas_call(
        functools.partial(body, T, B, COLS),
        out_shape=(
            jax.ShapeDtypeStruct((COLS, R), f32),
            jax.ShapeDtypeStruct((COLS, R), f32),
            jax.ShapeDtypeStruct((COLS, OL), f32),
        ),
        in_specs=[whole] + [far] * 7 + [whole],
        out_specs=(far, far, whole),
        scratch_shapes=scratch,
        compiler_params=pltpu.CompilerParams(
            collective_id=0, has_side_effects=True, vmem_limit_bytes=56 * 1024 * 1024
        ),
        cost_estimate=pl.CostEstimate(
            flops=2 * pairs * (D + COLS), bytes_accessed=8 * 1024 * 1024, transcendentals=2 * pairs
        ),
    )(
        batch_rows.reshape(steps * B * T, O), train_embed, lib_embed, labels[None, :],
        prior_draws, noise_draws, coefficients, velocity, library_prior,
    )


def solution(mesh):
    return jax.shard_map(
        functools.partial(per_device, mesh.shape["train"], mesh.shape["batch"]),
        mesh=mesh,
        in_specs=(
            P(),
            P("train", None),
            P("batch", None),
            P("train"),
            P(None, "train"),
            P(None, "train"),
            P(None, "train"),
            P(None, "train"),
            P(None, ("batch", "train")),
        ),
        out_specs=(P(None, "train"), P(None, "train"), P(None, ("batch", "train"))),
        check_vma=False,
    )
```

```python
import functools
import math

import jax
import jax.numpy as jnp
from jax import lax
from jax.experimental import pallas as pl
from jax.experimental.pallas import tpu as pltpu
from jax.sharding import PartitionSpec as P

momentum = 0.9
step_rate = 0.1
noise_var = 0.5
noise_scale = 0.7071067811865476
length_sq = 0.088

f32 = jnp.float32
bf16 = jnp.bfloat16
BLOCK = 1024
NORM_BLOCK = 256


def dot(a, b):
    return lax.dot_general(a, b, (((1,), (0,)), ((), ())), preferred_element_type=f32)


def dot_t(a, b):
    return lax.dot_general(a, b, (((1,), (1,)), ((), ())), preferred_element_type=f32)


def body(
    T, B, COLS,
    rows_ref, embed_hbm, lib_hbm, labels_hbm, prior_hbm, noise_hbm, coef_hbm, vel_hbm,
    newc_hbm, newv_hbm, pred_ref,
    embed, lib, labels, prior, noise, coef, vel, outc, outv,
    norms, hot0, hot1, wide, targets, w_first, w_base,
    qbuf, qt, acc, acc_lib, keys0, keys1, part2, part_l0, part_l1, overlap, own_terms,
    rs_send, rs_recv, rl_send, rl_recv, ag, gall,
    in_sem, out_sem, q_send, q_recv, f_send, f_recv, rs_ss, rs_rs, ag_ss, ag_rs,
):
    t = lax.axis_index("train")
    b = lax.axis_index("batch")
    R, D = embed.shape
    CP = acc.shape[0]
    O = ag.shape[3]
    OL = rl_send.shape[2]
    H = T // 2
    hots = (hot0, hot1)
    alpha = math.sqrt(5.0 / (length_sq * D))
    c1 = 1.5 / alpha
    c2 = 0.75 / (alpha * alpha)
    kappa = alpha * alpha / 3.0

    ins = []
    for i, (src, dst) in enumerate(
        (
            (embed_hbm, embed), (lib_hbm, lib), (coef_hbm, coef), (vel_hbm, vel),
            (labels_hbm, labels), (prior_hbm, prior), (noise_hbm, noise),
        )
    ):
        copy = pltpu.make_async_copy(src, dst, in_sem.at[i])
        copy.start()
        ins.append(copy)

    barrier = pltpu.get_barrier_semaphore()
    for d in range(1, T):
        pl.semaphore_signal(
            barrier, inc=1, device_id={"train": lax.rem(t + d, T)},
            device_id_type=pl.DeviceIdType.MESH,
        )
    for d in range(1, B):
        pl.semaphore_signal(
            barrier, inc=1, device_id={"batch": lax.rem(b + d, B)},
            device_id_type=pl.DeviceIdType.MESH,
        )

    base_row = (t * R).astype(f32)
    span = max(O, 128)
    slots = lax.broadcasted_iota(jnp.int32, (O, span), 0)
    lanes = lax.broadcasted_iota(jnp.int32, (O, span), 1)

    def build_hot(s, d):
        group = lax.rem(b + B - d, B)
        first = (group * T + t) * O
        chunk = first // span
        run = rows_ref[s : s + 1, pl.ds(pl.multiple_of(chunk * span, span), span)]
        picked = lanes == slots + (first - chunk * span)
        column = jnp.sum(
            jnp.where(picked, run.astype(f32) - base_row, 0.0), axis=1, keepdims=True
        ).astype(jnp.int32)
        lane = lax.broadcasted_iota(jnp.int32, (O, R), 1)
        hots[s][d * O : (d + 1) * O, :] = jnp.where(column == lane, 1.0, 0.0).astype(bf16)

    def remote(src, dst, ss, rs, axis, peer):
        return pltpu.make_async_remote_copy(
            src_ref=src, dst_ref=dst, send_sem=ss, recv_sem=rs,
            device_id={axis: peer}, device_id_type=pl.DeviceIdType.MESH,
        )

    sibling = t + 1 - 2 * lax.rem(t, 2)
    sends = []

    def q_direct(s, d):
        return remote(
            qbuf.at[s, t], qbuf.at[s, t], q_send.at[s, d], q_recv.at[s, d],
            "train", lax.rem(t + 2 * d, T),
        )

    def q_direct_recv(s, d):
        slot = lax.rem(t + T - 2 * d, T)
        remote(
            qbuf.at[s, slot], qbuf.at[s, slot], q_send.at[s, d], q_recv.at[s, d],
            "train", slot,
        ).wait_recv()

    def q_forward(s, d):
        slot = lax.rem(t + T - 2 * d, T)
        return remote(
            qbuf.at[s, slot], qbuf.at[s, slot], f_send.at[s, d], f_recv.at[s, d],
            "train", sibling,
        )

    def q_forward_recv(s, d):
        slot = lax.rem(sibling + T - 2 * d, T)
        remote(
            qbuf.at[s, slot], qbuf.at[s, slot], f_send.at[s, d], f_recv.at[s, d],
            "train", sibling,
        ).wait_recv()

    def start(copy):
        copy.start()
        sends.append(copy)

    def send_queries(s):
        for d in range(1, H):
            start(q_direct(s, d))
        start(q_forward(s, 0))

    def forward_queries(s):
        for d in range(1, H):
            q_direct_recv(s, d)
            start(q_forward(s, d))

    def finish_queries(s):
        for d in range(H):
            q_forward_recv(s, d)

    build_hot(0, 0)
    build_hot(1, 0)
    ins[0].wait()
    for s in range(2):
        qbuf[s, t] = dot(hots[s][0:O, :], embed[...]).astype(bf16)
    pl.semaphore_wait(barrier, T - 1 + B - 1)
    send_queries(0)

    def norm_block(i, _):
        at = pl.ds(pl.multiple_of(i * NORM_BLOCK, NORM_BLOCK), NORM_BLOCK)
        x = embed[at, :].astype(f32)
        norms[at, :] = jnp.broadcast_to(jnp.sum(x * x, axis=1, keepdims=True), (NORM_BLOCK, 128))
        return 0

    lax.fori_loop(0, R // NORM_BLOCK, norm_block, 0)

    ins[2].wait()
    ins[3].wait()
    wide[COLS - 1 : CP, :] = jnp.zeros((CP - COLS + 1, R), f32)
    wide[0:COLS, :] = coef[...] + momentum * (1.0 + momentum) * vel[...]
    w_base[...] = wide[...].astype(bf16)

    def query_side(q):
        qf = q.astype(f32).T
        qt[...] = (-2.0 * qf).astype(bf16)
        return jnp.sum(qf * qf, axis=0, keepdims=True)

    def kernel_block(keys, key_norms, query_norms):
        Q = query_norms.shape[1]
        wide_norms = jnp.concatenate([key_norms] * (Q // 128), axis=1)
        dist = jnp.maximum(dot(keys, qt[...]) + query_norms + wide_norms, 1e-20)
        root = dist * lax.rsqrt(dist)
        shifted = root + c1
        return ((shifted * shifted + c2) * jnp.exp(root * (-alpha))).astype(bf16)

    def apply_blocks(lower, upper, weights, query_norms, total):
        def step(i, _):
            at = pl.ds(pl.multiple_of(i * BLOCK, BLOCK), BLOCK)
            tile = kernel_block(embed[at, :], norms[at, :], query_norms)
            total[...] += dot(weights[:, at], tile)
            return 0

        lax.fori_loop(lower, upper, step, 0)

    def compact(keys, out, query_norms):
        x = keys[...].astype(f32)
        key_norms = jnp.broadcast_to(jnp.sum(x * x, axis=1, keepdims=True), (x.shape[0], 128))
        size = min(BLOCK, x.shape[0])
        for i in range(x.shape[0] // size):
            at = slice(i * size, (i + 1) * size)
            out[at, :] = kernel_block(keys[at, :], key_norms[at, :], query_norms)

    def scatter_send(ph, value):
        send, recv, size = (rs_send.at[ph], rs_recv.at[ph], O) if ph < 2 else (rl_send, rl_recv, OL)
        for k in range(T):
            send[k] = value[:, k * size : (k + 1) * size].astype(bf16)
        for d in range(1, T):
            peer = lax.rem(t + d, T)
            start(
                remote(
                    send.at[peer], recv.at[d - 1], rs_ss.at[ph, d], rs_rs.at[ph, d], "train", peer
                )
            )

    def scatter_recv(ph):
        send, recv = (rs_send.at[ph], rs_recv.at[ph]) if ph < 2 else (rl_send, rl_recv)
        total = send[t].astype(f32)
        for d in range(1, T):
            remote(
                send.at[0], recv.at[d - 1], rs_ss.at[ph, d], rs_rs.at[ph, d],
                "train", lax.rem(t + d, T),
            ).wait_recv()
            total = total + recv[d - 1].astype(f32)
        return total

    def share(ph, value):
        ag[ph, 0] = value.astype(bf16)
        for d in range(1, B):
            start(
                remote(
                    ag.at[ph, 0], ag.at[ph, d], ag_ss.at[ph, d], ag_rs.at[ph, d],
                    "batch", lax.rem(b + d, B),
                )
            )

    def collect(ph):
        for d in range(1, B):
            remote(
                ag.at[ph, 0], ag.at[ph, d], ag_ss.at[ph, d], ag_rs.at[ph, d],
                "batch", lax.rem(b + d, B),
            ).wait_recv()
        for d in range(B):
            gall[ph, :, d * O : (d + 1) * O] = ag[ph, d]

    blocks = R // BLOCK
    half = blocks // 2

    ins[1].wait()
    acc_lib[...] = jnp.zeros_like(acc_lib)
    lib_norms = query_side(lib[...])
    apply_blocks(0, half // 2, w_base, lib_norms, acc_lib)

    ins[4].wait()
    ins[5].wait()
    ins[6].wait()
    targets[COLS - 1 : CP, :] = jnp.zeros((CP - COLS + 1, R), f32)
    targets[0:1, :] = labels[...]
    targets[1:COLS, :] = labels[...] - prior[...] - noise_scale * noise[...]

    def own_term(s):
        value = noise_var * wide[...] - targets[...]
        high = value.astype(bf16)
        low = (value - high.astype(f32)).astype(bf16)
        own = hots[s][0:O, :]
        own_terms[s] = dot_t(high, own) + dot_t(low, own)

    own_term(1)
    wide[0:COLS, :] = coef[...] + momentum * vel[...]
    w_first[...] = wide[...].astype(bf16)
    own_term(0)
    for d in range(1, B):
        build_hot(0, d)
    keys0[...] = dot(hot0[...], embed[...]).astype(bf16)
    overlap[...] = dot_t(hot0[...], hot1[0:O, :]).astype(bf16)

    forward_queries(0)
    send_queries(1)
    apply_blocks(half // 2, half, w_base, lib_norms, acc_lib)
    finish_queries(0)

    acc[...] = jnp.zeros_like(acc)
    first_norms = query_side(qbuf[0].reshape(T * O, D))
    apply_blocks(0, blocks, w_first, first_norms, acc)
    scatter_send(0, kappa * acc[...])
    forward_queries(1)
    for d in range(1, B):
        build_hot(1, d)
    keys1[...] = dot(hot1[...], embed[...]).astype(bf16)
    finish_queries(1)

    acc[...] = jnp.zeros_like(acc)
    second_norms = query_side(qbuf[1].reshape(T * O, D))
    apply_blocks(0, half, w_base, second_norms, acc)
    share(0, scatter_recv(0) + own_terms[0])
    apply_blocks(half, blocks, w_base, second_norms, acc)
    compact(keys0, part2, second_norms)
    collect(0)
    g0 = gall[0]
    look = step_rate * (1.0 + momentum)
    scatter_send(1, kappa * (acc[...] - look * dot(g0, part2[...])))
    own_terms[1] = own_terms[1] - (noise_var * look) * dot(g0, overlap[...])

    lib_norms = query_side(lib[...])
    mid = half + half // 2
    apply_blocks(half, mid, w_base, lib_norms, acc_lib)
    share(1, scatter_recv(1) + own_terms[1])
    apply_blocks(mid, blocks, w_base, lib_norms, acc_lib)
    compact(keys0, part_l0, lib_norms)
    compact(keys1, part_l1, lib_norms)
    acc_lib[...] -= look * dot(g0, part_l0[...])
    collect(1)
    g1 = gall[1]
    scatter_send(2, kappa * (acc_lib[...] - step_rate * dot(g1, part_l1[...])))

    CH = min(R, 1024)
    for i in range(R // CH):
        at = slice(i * CH, (i + 1) * CH)
        grad0 = dot(g0, hot0[:, at])[0:COLS]
        grad1 = dot(g1, hot1[:, at])[0:COLS]
        v1 = momentum * vel[:, at] - step_rate * grad0
        v2 = momentum * v1 - step_rate * grad1
        outv[:, at] = v2
        outc[:, at] = (coef[:, at] + v1) + v2
    out_c = pltpu.make_async_copy(outc, newc_hbm, out_sem.at[0])
    out_v = pltpu.make_async_copy(outv, newv_hbm, out_sem.at[1])
    out_c.start()
    out_v.start()

    pred_ref[...] = scatter_recv(2)[0:COLS]
    out_c.wait()
    out_v.wait()
    for copy in sends:
        copy.wait_send()


def finish(c_ref, v_ref, total_ref, shift_ref, newc_ref, newv_ref, pred_ref):
    newc_ref[...] = c_ref[...]
    newv_ref[...] = v_ref[...]
    total = total_ref[...]
    pred_ref[0:1, :] = total[0:1]
    pred_ref[1:, :] = total[1:] + shift_ref[...]


def per_device(
    T, B,
    batch_rows, train_embed, lib_embed, labels, prior_draws, noise_draws,
    coefficients, velocity, library_prior,
):
    steps, batch = batch_rows.shape
    O = batch // (B * T)
    R, D = train_embed.shape
    COLS = coefficients.shape[0]
    CP = -(-COLS // 16) * 16
    LQ = lib_embed.shape[0]
    OL = LQ // T
    Q = T * O
    vmem = lambda *shape, dtype=f32: pltpu.VMEM(shape, dtype)
    dma = lambda *shape: pltpu.SemaphoreType.DMA(shape)
    whole = pl.BlockSpec(memory_space=pltpu.VMEM)
    far = pl.BlockSpec(memory_space=pl.ANY)
    scratch = [
        vmem(R, D, dtype=bf16), vmem(LQ, D, dtype=bf16), vmem(1, R), vmem(COLS - 1, R),
        vmem(COLS - 1, R), vmem(COLS, R), vmem(COLS, R), vmem(COLS, R), vmem(COLS, R),
        vmem(R, 128), vmem(B * O, R, dtype=bf16), vmem(B * O, R, dtype=bf16),
        vmem(CP, R), vmem(CP, R), vmem(CP, R, dtype=bf16), vmem(CP, R, dtype=bf16),
        vmem(2, T, O, D, dtype=bf16), vmem(D, Q, dtype=bf16), vmem(CP, Q), vmem(CP, LQ),
        vmem(B * O, D, dtype=bf16), vmem(B * O, D, dtype=bf16),
        vmem(B * O, Q, dtype=bf16), vmem(B * O, LQ, dtype=bf16), vmem(B * O, LQ, dtype=bf16),
        vmem(B * O, O, dtype=bf16), vmem(2, CP, O),
        vmem(2, T, CP, O, dtype=bf16), vmem(2, T - 1, CP, O, dtype=bf16),
        vmem(T, CP, OL, dtype=bf16), vmem(T - 1, CP, OL, dtype=bf16),
        vmem(2, B, CP, O, dtype=bf16), vmem(2, CP, B * O, dtype=bf16),
        dma(7), dma(2), dma(2, T), dma(2, T), dma(2, T), dma(2, T),
        dma(3, T), dma(3, T), dma(2, B), dma(2, B),
    ]
    pairs = (2 * Q + LQ) * R
    out_shape = (
        jax.ShapeDtypeStruct((COLS, R), f32),
        jax.ShapeDtypeStruct((COLS, R), f32),
        jax.ShapeDtypeStruct((COLS, OL), f32),
    )
    parts = pl.pallas_call(
        functools.partial(body, T, B, COLS),
        out_shape=out_shape,
        in_specs=[whole] + [far] * 7,
        out_specs=(far, far, whole),
        scratch_shapes=scratch,
        compiler_params=pltpu.CompilerParams(
            collective_id=0, has_side_effects=True, vmem_limit_bytes=56 * 1024 * 1024
        ),
        cost_estimate=pl.CostEstimate(
            flops=2 * pairs * (D + COLS), bytes_accessed=8 * 1024 * 1024, transcendentals=2 * pairs
        ),
    )(
        batch_rows, train_embed, lib_embed, labels[None, :],
        prior_draws, noise_draws, coefficients, velocity,
    )
    return pl.pallas_call(
        finish,
        out_shape=out_shape,
        in_specs=[whole] * 4,
        out_specs=(whole, whole, whole),
        compiler_params=pltpu.CompilerParams(vmem_limit_bytes=16 * 1024 * 1024),
    )(*parts, library_prior)


def solution(mesh):
    return jax.shard_map(
        functools.partial(per_device, mesh.shape["train"], mesh.shape["batch"]),
        mesh=mesh,
        in_specs=(
            P(),
            P("train", None),
            P("batch", None),
            P("train"),
            P(None, "train"),
            P(None, "train"),
            P(None, "train"),
            P(None, "train"),
            P(None, ("batch", "train")),
        ),
        out_specs=(P(None, "train"), P(None, "train"), P(None, ("batch", "train"))),
        check_vma=False,
    )
```
